32 devices in a mesh: dp: 16 (over z, y, core), seq: 2 (over x).
Axes of the slice: x: 2, y: 2, z: 4, core: 2. Of those that a mesh axis runs over, the one named last changes fastest.
Arguments:
- tokens: bfloat16 [16, 1024, 1024], P('dp', 'seq'), may hold values from -6 to 6
- cotangent: bfloat16 [16, 1024, 1024], P('dp', 'seq'), may hold values from -6 to 6
- attend_in: float32 [1024, 4096], P(('dp', 'seq')), may hold values from -0.1875 to 0.1875
- attend_in_first: float32 [1024, 4096], P(('dp', 'seq')), may hold values from -40 to 40
- attend_in_second: float32 [1024, 4096], P(('dp', 'seq')), may hold values from 32.768 to 131.072
- attend_out: float32 [2048, 1024], P(('dp', 'seq')), may hold values from -0.5 to 0.5
- attend_out_first: float32 [2048, 1024], P(('dp', 'seq')), may hold values from -40 to 40
- attend_out_second: float32 [2048, 1024], P(('dp', 'seq')), may hold values from 40.96 to 163.84
- gate_up: float32 [1024, 6144], P(('dp', 'seq')), may hold values from -0.1875 to 0.1875
- gate_up_first: float32 [1024, 6144], P(('dp', 'seq')), may hold values from -40 to 40
- gate_up_second: float32 [1024, 6144], P(('dp', 'seq')), may hold values from 16.384 to 65.536
- down_weight: float32 [3072, 1024], P(('dp', 'seq')), may hold values from -0.109375 to 0.109375
- down_first: float32 [3072, 1024], P(('dp', 'seq')), may hold values from -40 to 40
- down_second: float32 [3072, 1024], P(('dp', 'seq')), may hold values from 40.96 to 163.84
- norm_gains: float32 [2, 1024], P(None, ('dp', 'seq')), may hold values from 0.5 to 1.5
- norm_first: float32 [2, 1024], P(None, ('dp', 'seq')), may hold values from -192 to 192
- norm_second: float32 [2, 1024], P(None, ('dp', 'seq')), may hold values from 491.52 to 1966.08
- head_gains: float32 [256], P(('dp', 'seq')), may hold values from 0.5 to 1.5
- head_first: float32 [256], P(('dp', 'seq')), may hold values from -192 to 192
- head_second: float32 [256], P(('dp', 'seq')), may hold values from 491.52 to 1966.08
Outputs:
- activations: bfloat16 [16, 1024, 1024], P('dp', 'seq')
- input_grad: float32 [16, 1024, 1024], P('dp', 'seq')
- attend_in_grad: float32 [1024, 4096], P(('dp', 'seq'))
- attend_in_next: float32 [1024, 4096], P(('dp', 'seq'))
- attend_in_first_next: float32 [1024, 4096], P(('dp', 'seq'))
- attend_in_second_next: float32 [1024, 4096], P(('dp', 'seq'))
- attend_out_grad: float32 [2048, 1024], P(('dp', 'seq'))
- attend_out_next: float32 [2048, 1024], P(('dp', 'seq'))
- attend_out_first_next: float32 [2048, 1024], P(('dp', 'seq'))
- attend_out_second_next: float32 [2048, 1024], P(('dp', 'seq'))
- gate_up_grad: float32 [1024, 6144], P(('dp', 'seq'))
- gate_up_next: float32 [1024, 6144], P(('dp', 'seq'))
- gate_up_first_next: float32 [1024, 6144], P(('dp', 'seq'))
- gate_up_second_next: float32 [1024, 6144], P(('dp', 'seq'))
- down_grad: float32 [3072, 1024], P(('dp', 'seq'))
- down_next: float32 [3072, 1024], P(('dp', 'seq'))
- down_first_next: float32 [3072, 1024], P(('dp', 'seq'))
- down_second_next: float32 [3072, 1024], P(('dp', 'seq'))
- norm_grad: float32 [2, 1024], P(None, ('dp', 'seq'))
- norm_step: float32 [2, 1024], P(None, ('dp', 'seq'))
- norm_first_next: float32 [2, 1024], P(None, ('dp', 'seq'))
- norm_second_next: float32 [2, 1024], P(None, ('dp', 'seq'))
- head_grad: float32 [256], P(('dp', 'seq'))
- head_step: float32 [256], P(('dp', 'seq'))
- head_first_next: float32 [256], P(('dp', 'seq'))
- head_second_next: float32 [256], P(('dp', 'seq'))
The draws below stay inside these ranges and needn't reach their ends.
All inputs are finite; a program needn't handle non-finite values.
Results may differ from the reference program's by a relative error of at most 0.014.
The reference program's roundings to bfloat16 on the way count: a program that leaves them out, or rounds other values in their place, can miss the bound.
Values may be sent and summed in bfloat16 or wider, within the bound.
A program may use at most 320 MiB of HBM per device.

```python
import math
import jax
import jax.numpy as jnp
from jax import lax

D = 1024
QUERY_HEADS = 16
KEY_VALUE_HEADS = 8
HEAD_WIDTH = 128
FF = 3072
SEQ_LEN = 1024
QKV = 4096
SEQS = 1
SEQ_TOTAL = 16
TOKENS = 16384


def level_of(rng, dims, pieces, smallest, largest):
    def one(axis_at, blocks):
        draws = jax.random.uniform(jax.random.fold_in(jax.random.fold_in(rng, 6), axis_at), (blocks,), jnp.float32, smallest / len(pieces), largest / len(pieces))
        return jnp.repeat(jnp.exp(draws), dims[axis_at] // blocks).reshape((-1,) + (1,) * (len(dims) - axis_at - 1))

    level = one(*pieces[0])
    for cut in pieces[1:]:
        level = level * one(*cut)
    return level


def centred(rng, shape, spread, bound, split=(), kind=jnp.bfloat16):
    entries = jax.random.normal(rng, shape, jnp.float32) * spread
    if len(split) > 0:
        entries = level_of(rng, shape, split, -0.22, 0.18) * entries
    return jnp.clip(entries, min=-bound, max=bound).astype(kind)


def setup_inputs(seed: int = 0) -> dict:
    key_list = jax.random.split(jax.random.key(seed), 21)
    return {
        "tokens": centred(key_list[0], (SEQ_TOTAL, SEQ_LEN, D), 1.0, 6.0, ((0, 16), (1, 2))),
        "cotangent": centred(key_list[1], (SEQ_TOTAL, SEQ_LEN, D), 1.0, 6.0, ((0, 16), (1, 2))),
        "attend_in": centred(key_list[2], (D, QKV), D ** -0.5, 0.1875, ((0, 32),), jnp.float32),
        "attend_in_first": centred(key_list[3], (D, QKV), (0.05 * TOKENS ** 0.5), 40.0, ((0, 32),), jnp.float32),
        "attend_in_second": jnp.clip(jnp.exp(math.log(131.072) - 1.3862944 * jax.random.uniform(key_list[4], (D, QKV), jnp.float32) ** level_of(key_list[4], (D, QKV), ((0, 32),), -0.2, 0.2)), 32.768, 131.072),
        "attend_out": centred(key_list[5], (QUERY_HEADS * HEAD_WIDTH, D), (QUERY_HEADS * HEAD_WIDTH // 16) ** -0.5, 0.5, ((0, 32),), jnp.float32),
        "attend_out_first": centred(key_list[6], (QUERY_HEADS * HEAD_WIDTH, D), (0.05 * TOKENS ** 0.5), 40.0, ((0, 32),), jnp.float32),
        "attend_out_second": jnp.clip(jnp.exp(math.log(163.84) - 1.3862944 * jax.random.uniform(key_list[7], (QUERY_HEADS * HEAD_WIDTH, D), jnp.float32) ** level_of(key_list[7], (QUERY_HEADS * HEAD_WIDTH, D), ((0, 32),), -0.2, 0.2)), 40.96, 163.84),
        "gate_up": centred(key_list[8], (D, 2 * FF), D ** -0.5, 0.1875, ((0, 32),), jnp.float32),
        "gate_up_first": centred(key_list[9], (D, 2 * FF), (0.05 * TOKENS ** 0.5), 40.0, ((0, 32),), jnp.float32),
        "gate_up_second": jnp.clip(jnp.exp(math.log(65.536) - 1.3862944 * jax.random.uniform(key_list[10], (D, 2 * FF), jnp.float32) ** level_of(key_list[10], (D, 2 * FF), ((0, 32),), -0.2, 0.2)), 16.384, 65.536),
        "down_weight": centred(key_list[11], (FF, D), FF ** -0.5, 0.109375, ((0, 32),), jnp.float32),
        "down_first": centred(key_list[12], (FF, D), (0.05 * TOKENS ** 0.5), 40.0, ((0, 32),), jnp.float32),
        "down_second": jnp.clip(jnp.exp(math.log(163.84) - 1.3862944 * jax.random.uniform(key_list[13], (FF, D), jnp.float32) ** level_of(key_list[13], (FF, D), ((0, 32),), -0.2, 0.2)), 40.96, 163.84),
        "norm_gains": jnp.clip(1.0 + 0.1 * jax.random.normal(key_list[14], (2, D), jnp.float32), 0.5, 1.5),
        "norm_first": centred(key_list[15], (2, D), (0.25 * TOKENS ** 0.5), 192.0, ((1, 32),), jnp.float32),
        "norm_second": jnp.clip(jnp.exp(math.log(1966.08) - 1.3862944 * jax.random.uniform(key_list[16], (2, D), jnp.float32) ** level_of(key_list[16], (2, D), ((1, 32),), -0.2, 0.2)), 491.52, 1966.08),
        "head_gains": jnp.clip(1.0 + 0.1 * jax.random.normal(key_list[17], (2 * HEAD_WIDTH,), jnp.float32), 0.5, 1.5),
        "head_first": centred(key_list[18], (2 * HEAD_WIDTH,), (0.25 * TOKENS ** 0.5), 192.0, ((0, 32),), jnp.float32),
        "head_second": jnp.clip(jnp.exp(math.log(1966.08) - 1.3862944 * jax.random.uniform(key_list[19], (2 * HEAD_WIDTH,), jnp.float32) ** level_of(key_list[19], (2 * HEAD_WIDTH,), ((0, 32),), -0.2, 0.2)), 491.52, 1966.08),
    }


norm_eps = 1e-06
rope_base = 1000000.0
neg_fill = -1e+30
beta_one = 0.9
beta_two = 0.99
learn_rate = 0.02
weight_decay = 0.1
adam_eps = 1e-08

@jax.custom_vjp
def low(v):
    return lax.optimization_barrier(v.astype(jnp.bfloat16)).astype(jnp.float32)

@jax.custom_vjp
def low_back(v):
    return v

def low_keep(v):
    return (low(v), None)

def low_pass(kept, grad):
    return (grad,)

def back_keep(v):
    return (v, None)

def back_low(kept, grad):
    return (low(grad),)
low.defvjp(low_keep, low_pass)
low_back.defvjp(back_keep, back_low)

def matmul(left, right):
    return jnp.dot(left, right, precision=lax.Precision.HIGHEST, preferred_element_type=jnp.float32)

def rms_scale(values, gain):
    inverse = lax.rsqrt(lax.optimization_barrier(jnp.mean(values * values, -1, keepdims=True)) + norm_eps)
    return values * inverse * gain

def rotate(values, span_length):
    half_dim = HEAD_WIDTH // 2
    freq_index = jnp.arange(half_dim, dtype=jnp.float32)
    inverse_freq = rope_base ** (-2.0 * freq_index / HEAD_WIDTH)
    angles = jnp.arange(span_length, dtype=jnp.float32)[:, None] * inverse_freq[None, :]
    cosine = jnp.concatenate([jnp.cos(angles), jnp.cos(angles)], -1)[None, :, None, :]
    sine_table = jnp.concatenate([jnp.sin(angles), jnp.sin(angles)], -1)[None, :, None, :]
    turned = jnp.concatenate([-values[..., half_dim:], values[..., :half_dim]], -1)
    return values * cosine + turned * sine_table

def attend(block):
    query_rows, keys_gathered_full, values_gathered_full = block
    span_length = query_rows.shape[0]
    grouped_queries = query_rows.reshape(span_length, KEY_VALUE_HEADS, QUERY_HEADS // KEY_VALUE_HEADS, HEAD_WIDTH)
    scores = jnp.einsum('ckgd,lkd->kgcl', grouped_queries, keys_gathered_full, precision=lax.Precision.HIGHEST) * HEAD_WIDTH ** (-0.5)
    scores = low_back(scores)
    allowed = jnp.arange(span_length)[None, :] <= jnp.arange(span_length)[:, None]
    scores = jnp.where(allowed, scores, neg_fill)
    probs = low(jax.nn.softmax(scores, axis=-1))
    return jnp.einsum('kgcl,lkd->ckgd', probs, values_gathered_full, precision=lax.Precision.HIGHEST)

def forward(inputs, attend_in, attend_out, gate_up, down_weight, norm_gains, head_gains):
    sequence_count, span_length, width = inputs.shape
    flat_in = inputs.reshape(sequence_count * span_length, width)
    normed_one = low(rms_scale(flat_in, norm_gains[0]))
    joined_heads = low_back(matmul(normed_one, attend_in))
    query_columns = QUERY_HEADS * HEAD_WIDTH
    key_columns = KEY_VALUE_HEADS * HEAD_WIDTH
    query_rows = joined_heads[:, :query_columns].reshape(sequence_count, span_length, QUERY_HEADS, HEAD_WIDTH)
    keys_unnormed = joined_heads[:, query_columns:query_columns + key_columns].reshape(sequence_count, span_length, KEY_VALUE_HEADS, HEAD_WIDTH)
    values_unnormed = joined_heads[:, query_columns + key_columns:].reshape(sequence_count, span_length, KEY_VALUE_HEADS, HEAD_WIDTH)
    query_rot = rotate(rms_scale(query_rows, head_gains[:HEAD_WIDTH]), span_length)
    key_rot = rotate(rms_scale(keys_unnormed, head_gains[HEAD_WIDTH:]), span_length)
    query_narrowed = low_back(low(query_rot))
    key_low = low_back(low(key_rot))
    value_low = low_back(low(values_unnormed))
    mixed = lax.map(jax.checkpoint(attend), (query_narrowed, key_low, value_low))
    attn_low = low_back(low(mixed.reshape(sequence_count * span_length, query_columns)))
    middle = flat_in + low_back(matmul(attn_low, attend_out))
    normed_two = low(rms_scale(middle, norm_gains[1]))
    gate_values = low_back(matmul(normed_two, gate_up))
    hidden = low(jax.nn.silu(gate_values[:, :FF]) * gate_values[:, FF:])
    result = middle + low_back(matmul(hidden, down_weight))
    return result.reshape(sequence_count, span_length, width)

def adam_step(master, first_moment, second_moment, gradient):
    first_next = beta_one * first_moment + (1.0 - beta_one) * gradient
    second_next = beta_two * second_moment + (1.0 - beta_two) * gradient * gradient
    stride = first_next / (jnp.sqrt(second_next) + adam_eps) + weight_decay * master
    return (master - learn_rate * stride, first_next, second_next)

def gain_step(first_moment, second_moment, gradient):
    first_next = beta_one * first_moment + (1.0 - beta_one) * gradient
    second_next = beta_two * second_moment + (1.0 - beta_two) * gradient * gradient
    return (first_next / (jnp.sqrt(second_next) + adam_eps), first_next, second_next)

def reference(tokens, cotangent, attend_in, attend_in_first, attend_in_second, attend_out, attend_out_first, attend_out_second, gate_up, gate_up_first, gate_up_second, down_weight, down_first, down_second, norm_gains, norm_first, norm_second, head_gains, head_first, head_second):
    masters = (attend_in, attend_out, gate_up, down_weight, norm_gains, head_gains)
    rounded = tuple((low(item) for item in masters))
    groups = SEQ_TOTAL // SEQS
    inputs = tokens.astype(jnp.float32).reshape(groups, SEQS, SEQ_LEN, D)
    grads_in = cotangent.astype(jnp.float32).reshape(groups, SEQS, SEQ_LEN, D)

    def step(totals, batch):
        group_in, group_grad = batch
        outputs, pull = jax.vjp(forward, group_in, *rounded)
        pulled = pull(group_grad)
        totals = tuple((total + part for total, part in zip(totals, pulled[1:])))
        return (totals, (outputs.astype(jnp.bfloat16), pulled[0]))
    zeros_init = tuple((jnp.zeros(item.shape, jnp.float32) for item in masters))
    totals, (outputs, input_grads) = lax.scan(step, zeros_init, (inputs, grads_in))
    activations = outputs.reshape(SEQ_TOTAL, SEQ_LEN, D)
    input_grad = input_grads.reshape(SEQ_TOTAL, SEQ_LEN, D)
    in_grad, out_grad, gate_grad, down_grad, norm_grad, head_grad = totals
    in_next, in_first, in_second = adam_step(attend_in, attend_in_first, attend_in_second, in_grad)
    out_next, out_first, out_second = adam_step(attend_out, attend_out_first, attend_out_second, out_grad)
    gate_next, gate_first, gate_second = adam_step(gate_up, gate_up_first, gate_up_second, gate_grad)
    down_next, down_first_next, down_second_next = adam_step(down_weight, down_first, down_second, down_grad)
    norm_step, norm_first_next, norm_second_next = gain_step(norm_first, norm_second, norm_grad)
    head_step, head_first_next, head_second_next = gain_step(head_first, head_second, head_grad)
    return (activations, input_grad, in_grad, in_next, in_first, in_second, out_grad, out_next, out_first, out_second, gate_grad, gate_next, gate_first, gate_second, down_grad, down_next, down_first_next, down_second_next, norm_grad, norm_step, norm_first_next, norm_second_next, head_grad, head_step, head_first_next, head_second_next)
```

```python
import jax
import jax.numpy as jnp
from jax import lax
from jax.sharding import PartitionSpec as P

QUERY_HEADS = 16
KEY_VALUE_HEADS = 8
HEAD_WIDTH = 128
FF = 3072


norm_eps = 1e-06
rope_base = 1000000.0
neg_fill = -1e30
beta_one = 0.9
beta_two = 0.99
learn_rate = 0.02
weight_decay = 0.1
adam_eps = 1e-08


def rope_tables(positions, head_dim):
    half_dim = head_dim // 2
    freq_index = jnp.arange(half_dim, dtype=jnp.float32)
    inverse_freq = rope_base ** (-2.0 * freq_index / head_dim)
    angles = positions.astype(jnp.float32)[:, None] * inverse_freq[None, :]
    cosine = jnp.concatenate([jnp.cos(angles), jnp.cos(angles)], -1)[:, None, :]
    sine_table = jnp.concatenate([jnp.sin(angles), jnp.sin(angles)], -1)[:, None, :]
    return (cosine, sine_table)


def head_norm(values, gain):
    inverse = lax.rsqrt(jnp.mean(values * values, -1, keepdims=True) + norm_eps)
    unit_values = values * inverse
    return (unit_values * gain, unit_values, inverse)


def rotate_forward(values, cosine, sine_table):
    half_dim = values.shape[-1] // 2
    turned = jnp.concatenate([-values[..., half_dim:], values[..., :half_dim]], -1)
    return values * cosine + turned * sine_table


def rotate_back(gradient, cosine, sine_table):
    half_dim = gradient.shape[-1] // 2
    scaled = gradient * sine_table
    return gradient * cosine + jnp.concatenate(
        [scaled[..., half_dim:], -scaled[..., :half_dim]], -1
    )


def norm_back(gradient, unit_values, inverse, gain):
    weighted = gradient * gain
    return inverse * (weighted - unit_values * jnp.mean(weighted * unit_values, -1, keepdims=True))


def masked_scores(query_rows, keys_gathered_full, offset):
    scale = query_rows.shape[-1] ** (-0.5)
    scores = (
        jnp.einsum(
            "ckgd,lkd->kgcl", query_rows, keys_gathered_full, preferred_element_type=jnp.float32
        )
        * scale
    )
    query_pos = offset + jnp.arange(query_rows.shape[0])
    allowed = jnp.arange(keys_gathered_full.shape[0])[None, :] <= query_pos[:, None]
    return jnp.where(allowed, scores, neg_fill)


def adam_step(master, first_moment, second_moment, gradient):
    first_next = beta_one * first_moment + (1.0 - beta_one) * gradient
    second_next = beta_two * second_moment + (1.0 - beta_two) * gradient * gradient
    stride = first_next / (jnp.sqrt(second_next) + adam_eps) + weight_decay * master
    return (master - learn_rate * stride, first_next, second_next)


def gain_step(first_moment, second_moment, gradient):
    first_next = beta_one * first_moment + (1.0 - beta_one) * gradient
    second_next = beta_two * second_moment + (1.0 - beta_two) * gradient * gradient
    return (first_next / (jnp.sqrt(second_next) + adam_eps), first_next, second_next)


def axis_bits():
    bits = []
    for name in ("dp", "seq"):
        count = lax.axis_size(name).bit_length() - 1
        bits += [(name, bit) for bit in range(count - 1, -1, -1)]
    return bits


def swap(value, bit):
    name, place = bit
    pairs = [(i, i ^ (1 << place)) for i in range(lax.axis_size(name))]
    return lax.ppermute(value, name, pairs)


def own_bit(bit):
    name, place = bit
    return (lax.axis_index(name) >> place) & 1


def halving_order(y_first):
    rest = [b for b in axis_bits() if b not in (("dp", 0), ("dp", 1)) and b[0] == "dp"]
    seq = [b for b in axis_bits() if b[0] == "seq"]
    near, mid = [("dp", 0)], [("dp", 1)]
    middle = mid + seq if y_first else seq + mid
    return near + middle + rest[::-1]


def scatter_sum(terms, order, wire):
    bits = [b for b in axis_bits() if b in order]
    rows = terms.shape[0] >> len(bits)
    held = terms.reshape((2,) * len(bits) + (rows,) + terms.shape[1:])
    left = list(bits)
    for bit in order:
        at = left.index(bit)
        mine = own_bit(bit)
        keep = lax.dynamic_index_in_dim(held, mine, at, keepdims=False)
        send = lax.dynamic_index_in_dim(held, 1 - mine, at, keepdims=False).astype(wire)
        held = keep + swap(send, bit).astype(jnp.float32)
        left.remove(bit)
    return held


def gather_rows(shard, order, busy):
    bits = [b for b in axis_bits() if b in order]
    held = shard
    have = []
    for bit in order[::-1]:
        if bit in busy:
            held, _ = lax.optimization_barrier((held, busy[bit]))
        got = swap(held, bit)
        busy[bit] = got
        have = [b for b in bits if b in have or b == bit]
        mine = own_bit(bit) == 0
        held = jnp.stack(
            [jnp.where(mine, held, got), jnp.where(mine, got, held)], have.index(bit)
        )
    return held.reshape((-1,) + shard.shape[1:])


def body(
    tokens,
    cotangent,
    attend_in,
    attend_in_first,
    attend_in_second,
    attend_out,
    attend_out_first,
    attend_out_second,
    gate_up,
    gate_up_first,
    gate_up_second,
    down_weight,
    down_first,
    down_second,
    norm_gains,
    norm_first,
    norm_second,
    head_gains,
    head_first,
    head_second,
):
    narrow_dtype = jnp.bfloat16
    sequence_count, window_length, width = tokens.shape
    token_rows = sequence_count * window_length
    heads_per_group = QUERY_HEADS // KEY_VALUE_HEADS
    query_columns = QUERY_HEADS * HEAD_WIDTH
    key_columns = KEY_VALUE_HEADS * HEAD_WIDTH
    sequence_length = window_length * lax.axis_size("seq")
    in_low = attend_in.astype(narrow_dtype)
    out_low = attend_out.astype(narrow_dtype)
    gate_low = gate_up.astype(narrow_dtype)
    down_low = down_weight.astype(narrow_dtype)
    x_first = halving_order(False)
    y_first = halving_order(True)
    along_seq = [b for b in x_first if b[0] == "seq"]
    shards = lax.axis_size("dp") * lax.axis_size("seq")
    norm_part = norm_gains.shape[1]
    head_part = head_gains.shape[0]
    gains = jnp.concatenate([norm_gains[0], norm_gains[1], head_gains]).astype(narrow_dtype)
    gains = jnp.pad(gains, (0, -gains.shape[0] % 128))[None]
    gains_full = gather_rows(gains, x_first, {})
    norm_full = jnp.stack(
        [
            gains_full[:, :norm_part].reshape(width),
            gains_full[:, norm_part : 2 * norm_part].reshape(width),
        ]
    )
    head_full = gains_full[:, 2 * norm_part : 2 * norm_part + head_part].reshape(2 * HEAD_WIDTH)
    busy = {}
    in_query = gather_rows(in_low[:, :query_columns], x_first, busy)
    in_key_value = gather_rows(in_low[:, query_columns:], y_first, busy)
    out_full = gather_rows(out_low, x_first, busy)
    gate_first_half = gather_rows(gate_low[:, :FF], y_first, busy)
    gate_second_half = gather_rows(gate_low[:, FF:], x_first, busy)
    down_full = gather_rows(down_low, y_first, busy)
    norm_vals = norm_full.astype(jnp.float32)
    head_vals = head_full.astype(jnp.float32)
    flat_in = tokens.reshape(token_rows, width).astype(jnp.float32)
    inverse_one = lax.rsqrt(jnp.mean(flat_in * flat_in, -1, keepdims=True) + norm_eps)
    unit_one = flat_in * inverse_one
    normed_one = (unit_one * norm_vals[0]).astype(narrow_dtype)
    query_raw = jnp.dot(normed_one, in_query, preferred_element_type=jnp.float32)
    query_raw = query_raw.reshape(token_rows, QUERY_HEADS, HEAD_WIDTH)
    key_value = jnp.dot(normed_one, in_key_value, preferred_element_type=jnp.float32)
    key_unnormed = key_value[:, :key_columns].reshape(token_rows, KEY_VALUE_HEADS, HEAD_WIDTH)
    value_low = key_value[:, key_columns:].astype(narrow_dtype)
    offset = lax.axis_index("seq") * window_length
    positions = jnp.tile(offset + jnp.arange(window_length), sequence_count)
    cosine, sine_table = rope_tables(positions, HEAD_WIDTH)
    query_normed, query_unit, query_inverse = head_norm(query_raw, head_vals[:HEAD_WIDTH])
    key_normed, key_unit, key_inverse = head_norm(key_unnormed, head_vals[HEAD_WIDTH:])
    query_narrowed = rotate_forward(query_normed, cosine, sine_table).astype(narrow_dtype)
    key_low = rotate_forward(key_normed, cosine, sine_table).astype(narrow_dtype)
    both_low = jnp.stack([key_low.reshape(token_rows, key_columns), value_low])
    both_full = gather_rows(
        both_low.reshape(1, 2, sequence_count, window_length, key_columns), along_seq, {}
    )
    keys_gathered_full = jnp.moveaxis(both_full[:, 0], 0, 1)
    values_gathered_full = jnp.moveaxis(both_full[:, 1], 0, 1)
    keys_gathered_full = keys_gathered_full.reshape(
        sequence_count, sequence_length, KEY_VALUE_HEADS, HEAD_WIDTH
    )
    values_gathered_full = values_gathered_full.reshape(
        sequence_count, sequence_length, KEY_VALUE_HEADS, HEAD_WIDTH
    )
    query_head_groups = query_narrowed.reshape(
        sequence_count, window_length, KEY_VALUE_HEADS, heads_per_group, HEAD_WIDTH
    )

    def attend_forward(block):
        query_rows, keys_seq, values_seq = block
        scores = masked_scores(query_rows, keys_seq, offset)
        top_score = jnp.max(scores, -1, keepdims=True)
        expo = jnp.exp(scores - top_score)
        total = jnp.sum(expo, -1, keepdims=True)
        probs = expo / total
        mixed = jnp.einsum(
            "kgcl,lkd->ckgd",
            probs.astype(narrow_dtype),
            values_seq,
            preferred_element_type=jnp.float32,
        )
        return (mixed, top_score + jnp.log(total))

    mixed, log_totals = lax.map(
        attend_forward, (query_head_groups, keys_gathered_full, values_gathered_full)
    )
    attn_low = mixed.reshape(token_rows, query_columns).astype(narrow_dtype)
    middle = flat_in + jnp.dot(attn_low, out_full, preferred_element_type=jnp.float32)
    inverse_two = lax.rsqrt(jnp.mean(middle * middle, -1, keepdims=True) + norm_eps)
    unit_two = middle * inverse_two
    normed_two = (unit_two * norm_vals[1]).astype(narrow_dtype)
    gate_part = jnp.dot(normed_two, gate_first_half, preferred_element_type=jnp.float32)
    up_part = jnp.dot(normed_two, gate_second_half, preferred_element_type=jnp.float32)
    sigma_gate = jax.nn.sigmoid(gate_part)
    silu_gate = gate_part * sigma_gate
    hidden_low = (silu_gate * up_part).astype(narrow_dtype)
    result = middle + jnp.dot(hidden_low, down_full, preferred_element_type=jnp.float32)
    activations = result.astype(narrow_dtype).reshape(tokens.shape)
    grad_rows = cotangent.reshape(token_rows, width)
    grad_float = grad_rows.astype(jnp.float32)
    down_grad_local = jnp.einsum(
        "tf,td->fd", hidden_low, grad_rows, preferred_element_type=jnp.float32
    )
    hidden_grad = jnp.einsum("td,fd->tf", grad_rows, down_full, preferred_element_type=jnp.float32)
    gate_grad_part = hidden_grad * up_part * sigma_gate * (1.0 + gate_part * (1.0 - sigma_gate))
    up_grad_part = hidden_grad * silu_gate
    down_grad = scatter_sum(down_grad_local, x_first, narrow_dtype)
    gate_grad_low = gate_grad_part.astype(narrow_dtype)
    up_grad_low = up_grad_part.astype(narrow_dtype)
    gate_grad = jnp.concatenate(
        [
            scatter_sum(
                jnp.einsum("td,tf->df", normed_two, part, preferred_element_type=jnp.float32),
                order,
                narrow_dtype,
            )
            for part, order in ((gate_grad_low, y_first), (up_grad_low, x_first))
        ],
        1,
    )
    normed_two_grad = jnp.einsum(
        "tf,df->td", gate_grad_low, gate_first_half, preferred_element_type=jnp.float32
    ) + jnp.einsum("tf,df->td", up_grad_low, gate_second_half, preferred_element_type=jnp.float32)
    norm_two_gain = jnp.sum(normed_two_grad * unit_two, 0)
    middle_grad = grad_float + norm_back(normed_two_grad, unit_two, inverse_two, norm_vals[1])
    attn_grad = middle_grad.astype(narrow_dtype)
    out_grad_local = jnp.einsum(
        "tq,td->qd", attn_low, attn_grad, preferred_element_type=jnp.float32
    )
    out_grad = scatter_sum(out_grad_local, y_first, narrow_dtype)
    narrow_gradient = jnp.einsum(
        "td,qd->tq", attn_grad, out_full, preferred_element_type=jnp.float32
    ).astype(narrow_dtype)
    narrow_gradient = narrow_gradient.reshape(
        sequence_count, window_length, KEY_VALUE_HEADS, heads_per_group, HEAD_WIDTH
    )

    def attend_backward(block):
        query_rows, keys_seq, values_seq, grad_mixed, log_total = block
        scale = query_rows.shape[-1] ** (-0.5)
        scores = masked_scores(query_rows, keys_seq, offset)
        probs = jnp.exp(scores - log_total)
        grad_probs = jnp.einsum(
            "ckgd,lkd->kgcl", grad_mixed, values_seq, preferred_element_type=jnp.float32
        )
        grad_scores = (
            probs * (grad_probs - jnp.sum(probs * grad_probs, -1, keepdims=True))
        ).astype(narrow_dtype)
        grad_query = (
            jnp.einsum("kgcl,lkd->ckgd", grad_scores, keys_seq, preferred_element_type=jnp.float32)
            * scale
        )
        grad_key = (
            jnp.einsum(
                "kgcl,ckgd->lkd", grad_scores, query_rows, preferred_element_type=jnp.float32
            )
            * scale
        )
        grad_value = jnp.einsum(
            "kgcl,ckgd->lkd",
            probs.astype(narrow_dtype),
            grad_mixed,
            preferred_element_type=jnp.float32,
        )
        return (grad_query, grad_key, grad_value)

    query_grads, key_terms, value_terms = lax.map(
        attend_backward,
        (query_head_groups, keys_gathered_full, values_gathered_full, narrow_gradient, log_totals),
    )
    both_terms = jnp.stack([key_terms, value_terms]).reshape(
        2, sequence_count, -1, window_length, key_columns
    )
    both_sums = scatter_sum(jnp.moveaxis(both_terms, 2, 0), along_seq, narrow_dtype)[0]
    key_row_sums, value_sums = both_sums[0], both_sums[1]
    key_narrowed = (
        key_row_sums.astype(narrow_dtype)
        .astype(jnp.float32)
        .reshape(token_rows, KEY_VALUE_HEADS, HEAD_WIDTH)
    )
    value_rounded = value_sums.astype(narrow_dtype).reshape(token_rows, key_columns)
    query_rounded = (
        query_grads.astype(narrow_dtype)
        .astype(jnp.float32)
        .reshape(token_rows, QUERY_HEADS, HEAD_WIDTH)
    )
    query_normed_grad = rotate_back(query_rounded, cosine, sine_table)
    key_normed_grad = rotate_back(key_narrowed, cosine, sine_table)
    query_gain_grad = jnp.sum(query_normed_grad * query_unit, (0, 1))
    key_gain_grad = jnp.sum(key_normed_grad * key_unit, (0, 1))
    query_raw_grad = norm_back(query_normed_grad, query_unit, query_inverse, head_vals[:HEAD_WIDTH])
    key_raw_grad = norm_back(key_normed_grad, key_unit, key_inverse, head_vals[HEAD_WIDTH:])
    query_in_grad = query_raw_grad.reshape(token_rows, query_columns).astype(narrow_dtype)
    key_value_in_grad = jnp.concatenate(
        [key_raw_grad.reshape(token_rows, key_columns).astype(narrow_dtype), value_rounded], -1
    )
    in_grad = jnp.concatenate(
        [
            scatter_sum(
                jnp.einsum("td,tq->dq", normed_one, part, preferred_element_type=jnp.float32),
                order,
                narrow_dtype,
            )
            for part, order in ((query_in_grad, x_first), (key_value_in_grad, y_first))
        ],
        1,
    )
    normed_one_grad = jnp.einsum(
        "tq,dq->td", query_in_grad, in_query, preferred_element_type=jnp.float32
    ) + jnp.einsum(
        "tq,dq->td", key_value_in_grad, in_key_value, preferred_element_type=jnp.float32
    )
    norm_one_gain = jnp.sum(normed_one_grad * unit_one, 0)
    input_grad = middle_grad + norm_back(normed_one_grad, unit_one, inverse_one, norm_vals[0])
    input_grad = input_grad.reshape(tokens.shape)
    gain_terms = jnp.concatenate(
        [
            norm_one_gain.reshape(shards, norm_part),
            norm_two_gain.reshape(shards, norm_part),
            jnp.concatenate([query_gain_grad, key_gain_grad]).reshape(shards, head_part),
        ],
        1,
    )
    gain_terms = jnp.pad(gain_terms, ((0, 0), (0, -gain_terms.shape[1] % 128)))
    gain_sums = scatter_sum(gain_terms, x_first, jnp.float32)[0]
    norm_grad = gain_sums[: 2 * norm_part].reshape(2, norm_part)
    head_grad = gain_sums[2 * norm_part : 2 * norm_part + head_part]
    in_next, in_first, in_second = adam_step(attend_in, attend_in_first, attend_in_second, in_grad)
    out_next, out_first, out_second = adam_step(
        attend_out, attend_out_first, attend_out_second, out_grad
    )
    gate_next, gate_first, gate_second = adam_step(
        gate_up, gate_up_first, gate_up_second, gate_grad
    )
    down_next, down_first_next, down_second_next = adam_step(
        down_weight, down_first, down_second, down_grad
    )
    norm_step, norm_first_next, norm_second_next = gain_step(norm_first, norm_second, norm_grad)
    head_step, head_first_next, head_second_next = gain_step(head_first, head_second, head_grad)
    return (
        activations,
        input_grad,
        in_grad,
        in_next,
        in_first,
        in_second,
        out_grad,
        out_next,
        out_first,
        out_second,
        gate_grad,
        gate_next,
        gate_first,
        gate_second,
        down_grad,
        down_next,
        down_first_next,
        down_second_next,
        norm_grad,
        norm_step,
        norm_first_next,
        norm_second_next,
        head_grad,
        head_step,
        head_first_next,
        head_second_next,
    )


def solution(mesh):
    in_specs = (
        P("dp", "seq", None),
        P("dp", "seq", None),
        P(("dp", "seq"), None),
        P(("dp", "seq"), None),
        P(("dp", "seq"), None),
        P(("dp", "seq"), None),
        P(("dp", "seq"), None),
        P(("dp", "seq"), None),
        P(("dp", "seq"), None),
        P(("dp", "seq"), None),
        P(("dp", "seq"), None),
        P(("dp", "seq"), None),
        P(("dp", "seq"), None),
        P(("dp", "seq"), None),
        P(None, ("dp", "seq")),
        P(None, ("dp", "seq")),
        P(None, ("dp", "seq")),
        P(("dp", "seq")),
        P(("dp", "seq")),
        P(("dp", "seq")),
    )
    out_specs = (
        P("dp", "seq", None),
        P("dp", "seq", None),
        P(("dp", "seq"), None),
        P(("dp", "seq"), None),
        P(("dp", "seq"), None),
        P(("dp", "seq"), None),
        P(("dp", "seq"), None),
        P(("dp", "seq"), None),
        P(("dp", "seq"), None),
        P(("dp", "seq"), None),
        P(("dp", "seq"), None),
        P(("dp", "seq"), None),
        P(("dp", "seq"), None),
        P(("dp", "seq"), None),
        P(("dp", "seq"), None),
        P(("dp", "seq"), None),
        P(("dp", "seq"), None),
        P(("dp", "seq"), None),
        P(None, ("dp", "seq")),
        P(None, ("dp", "seq")),
        P(None, ("dp", "seq")),
        P(None, ("dp", "seq")),
        P(("dp", "seq")),
        P(("dp", "seq")),
        P(("dp", "seq")),
        P(("dp", "seq")),
    )
    return jax.shard_map(body, mesh=mesh, in_specs=in_specs, out_specs=out_specs, check_vma=False)
```
